32 devices in a mesh: groups: 2 (over y), dom: 8 (over z, x), feat: 2 (over core).
Axes of the slice: x: 2, y: 2, z: 4, core: 2. Of those that a mesh axis runs over, the one named last changes fastest.
Arguments:
- mesh_nodes: bfloat16 [4096, 512], P(('groups', 'dom'), 'feat'), parts along dimension 0, may hold values from -6 to 6
- mesh_edges: bfloat16 [8192, 512], P(('groups', 'dom'), 'feat'), parts along dimension 0, may hold values from -6 to 6
- grid_nodes: bfloat16 [4096, 512], P(('groups', 'dom'), 'feat'), parts along dimension 0, may hold values from -6 to 6
- decoder_edges: bfloat16 [8192, 512], P(('groups', 'dom'), 'feat'), parts along dimension 0, may hold values from -6 to 6
- mesh_sender: int32 [8192], P(('groups', 'dom')), parts along dimension 0, may hold values from 0 to 271, as said below
- mesh_window: int32 [64], P(('groups', 'dom')), parts along dimension 0, may hold values from 0 to 128
- mesh_segment: int32 [8192], P(('groups', 'dom')), parts along dimension 0, may hold values from 0 to 128, as said below
- mesh_lists: int32 [16, 16], P(('groups', 'dom')), parts along dimension 0, may hold values from 0 to 255
- decoder_sender: int32 [8192], P(('groups', 'dom')), parts along dimension 0, may hold values from 0 to 31, as said below
- decoder_window: int32 [64], P(('groups', 'dom')), parts along dimension 0, may hold values from 0 to 128
- decoder_segment: int32 [8192], P(('groups', 'dom')), parts along dimension 0, may hold values from 0 to 128, as said below
- decoder_lists: int32 [16, 32], P(('groups', 'dom')), parts along dimension 0, may hold values from 0 to 255
- edge_first: bfloat16 [1536, 512], P(None, 'feat'), may hold values from -0.15625 to 0.15625
- edge_second: bfloat16 [512, 512], P('feat'), may hold values from -0.25 to 0.25
- edge_gain: float32 [512], replicated, may hold values from 0.1 to 1.9
- node_first: bfloat16 [1024, 512], P(None, 'feat'), may hold values from -0.1875 to 0.1875
- node_second: bfloat16 [512, 512], P('feat'), may hold values from -0.25 to 0.25
- node_gain: float32 [512], replicated, may hold values from 0.1 to 1.9
- decoder_first: bfloat16 [1536, 512], P(None, 'feat'), may hold values from -0.15625 to 0.15625
- decoder_second: bfloat16 [512, 512], P('feat'), may hold values from -0.25 to 0.25
- decoder_gain: float32 [512], replicated, may hold values from 0.1 to 1.9
- grid_first: bfloat16 [1024, 512], P(None, 'feat'), may hold values from -0.1875 to 0.1875
- grid_second: bfloat16 [512, 512], P('feat'), may hold values from -0.25 to 0.25
- grid_gain: float32 [512], replicated, may hold values from 0.1 to 1.9
Outputs:
- mesh_out: bfloat16 [4096, 512], P(('groups', 'dom'), 'feat'), parts along dimension 0
- grid_out: bfloat16 [4096, 512], P(('groups', 'dom'), 'feat'), parts along dimension 0
The draws below stay inside these ranges and needn't reach their ends.
There are 2 independent parts, one for each index of `groups`. The reference program is written for one: setup_inputs(seed, part) draws one part's arguments, and reference() takes and returns one part's arrays. A program takes and returns all parts, laid end to end along the dimension named above; an argument that names none is the same for every part. Nothing has to cross between parts.
Inputs may be any that keep to these rules, and one draw needn't show every extreme that they name: `mesh_sender`: slots below 256 name an own node of the edge's partition; a slot 256 + q * 2 + c names entry c of what partition q sends to this partition. Every slot is named by some edge of each partition. `mesh_segment`: 128 marks a padding edge; padding edges stand at the end of each partition's rows, and every partition has some. `decoder_sender`: A slot q * 4 + c names entry c of what partition q sends to this slab. Every slot is named by some edge of each slab. `decoder_segment`: 128 marks a padding edge; padding edges stand at the end of each slab's rows, and every slab has some.
All inputs are finite; a program needn't handle non-finite values.
Results may differ from the reference program's by a relative error of at most 0.0052.
Values may be sent and summed in bfloat16 or wider, within the bound.
A program may use at most 64 MiB of HBM per device.

```python
import jax
import jax.numpy as jnp
from jax import lax

LATENT = 512
BLOCK = 128
MESH_DEV = 256
EDGE_DEV = 512
GRID_DEV = 256
LINK_DEV = 512
MESH_CAP = 2
GRID_CAP = 4
PARTITIONS = 8
MESH = 2048
EDGES = 4096
GRID = 2048
LINKS = 4096
N_DOM = 8


def sender_slots(key, count, modulus):
    subkeys = jax.random.split(key, PARTITIONS)
    orders = jax.vmap(lambda subkey: jax.random.permutation(subkey, count))(subkeys)
    return (orders % modulus).reshape(-1).astype(jnp.int32)


def padded_segments(key, count):
    first_key, second_key = jax.random.split(key)
    live_count = jax.random.randint(first_key, (PARTITIONS, 1), count // 8, count)
    segment_ids = jax.random.randint(second_key, (PARTITIONS, count), 0, BLOCK)
    position = jnp.arange(count, dtype=jnp.int32)[None, :]
    return jnp.where(position < live_count, segment_ids, BLOCK).reshape(-1).astype(jnp.int32)


def draw_mesh_sender(key, part):
    key = jax.random.fold_in(key, 11)
    return sender_slots(key, EDGE_DEV, MESH_DEV + PARTITIONS * MESH_CAP)


def draw_mesh_segment(key, part):
    key = jax.random.fold_in(key, 12)
    return padded_segments(key, EDGE_DEV)


def draw_decoder_sender(key, part):
    key = jax.random.fold_in(key, 13)
    return sender_slots(key, LINK_DEV, PARTITIONS * GRID_CAP)


def draw_decoder_segment(key, part):
    key = jax.random.fold_in(key, 14)
    return padded_segments(key, LINK_DEV)


def set_ends(result, stream_key, smallest, top_value):
    dims = result.shape
    spot = [jax.random.randint(jax.random.fold_in(stream_key, axis), (), 0, dims[axis]) for axis in range(len(dims))]
    result = result.at[tuple(spot)].set(smallest)
    longest = dims.index(max(dims))
    spot[longest] = (spot[longest] + 1) % dims[longest]
    return result.at[tuple(spot)].set(top_value)


def shard_levels(own_key, extent, shards, least, top_value):
    def one(dim, shards_of):
        heights = jax.random.uniform(jax.random.fold_in(jax.random.fold_in(own_key, 6), dim), (shards_of,), jnp.float32, least / len(shards), top_value / len(shards))
        return jnp.repeat(jnp.exp(heights), extent[dim] // shards_of).reshape((-1,) + (1,) * (len(extent) - dim - 1))

    level = one(*shards[0])
    for cut in shards[1:]:
        level = level * one(*cut)
    return level


def normal_values(rng, shape, width, reach, cuts=(), kind=jnp.bfloat16):
    result = width * jax.random.normal(rng, shape, jnp.float32)
    if cuts:
        result = result * shard_levels(rng, shape, cuts, -0.22, 0.18)
    return jnp.clip(result, -reach, reach).astype(kind)


def setup_inputs(seed: int = 0, part: int = 0) -> dict:
    key_list = jax.random.split(jax.random.key(seed), 25)
    part_keys = jax.random.split(jax.random.fold_in(key_list[24], part), 25)
    mesh_nodes = normal_values(part_keys[0], (MESH, LATENT), 1.0, 6.0, ((0, 8), (1, 2)))
    mesh_edges = normal_values(part_keys[1], (EDGES, LATENT), 1.0, 6.0, ((0, 8), (1, 2)))
    grid_nodes = normal_values(part_keys[2], (GRID, LATENT), 1.0, 6.0, ((0, 8), (1, 2)))
    decoder_edges = normal_values(part_keys[3], (LINKS, LATENT), 1.0, 6.0, ((0, 8), (1, 2)))
    mesh_sender = draw_mesh_sender(jax.random.fold_in(jax.random.fold_in(key_list[24], part), 71), part)
    mesh_window = set_ends(jax.random.randint(part_keys[5], (EDGES // BLOCK,), 0, MESH_DEV - BLOCK + 1), jax.random.fold_in(part_keys[5], 1), 0, MESH_DEV - BLOCK).astype(jnp.int32)
    mesh_segment = draw_mesh_segment(jax.random.fold_in(jax.random.fold_in(key_list[24], part), 71), part)
    mesh_lists = set_ends(jax.random.randint(part_keys[7], (PARTITIONS, PARTITIONS * MESH_CAP), 0, MESH_DEV), jax.random.fold_in(part_keys[7], 1), 0, MESH_DEV - 1).astype(jnp.int32)
    decoder_sender = draw_decoder_sender(jax.random.fold_in(jax.random.fold_in(key_list[24], part), 71), part)
    decoder_window = set_ends(jax.random.randint(part_keys[9], (LINKS // BLOCK,), 0, GRID_DEV - BLOCK + 1), jax.random.fold_in(part_keys[9], 1), 0, GRID_DEV - BLOCK).astype(jnp.int32)
    decoder_segment = draw_decoder_segment(jax.random.fold_in(jax.random.fold_in(key_list[24], part), 71), part)
    decoder_lists = set_ends(jax.random.randint(part_keys[11], (PARTITIONS, PARTITIONS * GRID_CAP), 0, MESH_DEV), jax.random.fold_in(part_keys[11], 1), 0, MESH_DEV - 1).astype(jnp.int32)
    edge_first = normal_values(key_list[12], (3 * LATENT, LATENT), (3 * LATENT) ** -0.5, 0.15625, ((1, 2),))
    edge_second = normal_values(key_list[13], (LATENT, LATENT), LATENT ** -0.5, 0.25, ((0, 2),))
    edge_gain = jnp.clip(1.0 + 0.18 * jax.random.normal(key_list[14], (LATENT,), jnp.float32), 0.1, 1.9)
    node_first = normal_values(key_list[15], (2 * LATENT, LATENT), (2 * LATENT) ** -0.5, 0.1875, ((1, 2),))
    node_second = normal_values(key_list[16], (LATENT, LATENT), LATENT ** -0.5, 0.25, ((0, 2),))
    node_gain = jnp.clip(1.0 + 0.18 * jax.random.normal(key_list[17], (LATENT,), jnp.float32), 0.1, 1.9)
    decoder_first = normal_values(key_list[18], (3 * LATENT, LATENT), (3 * LATENT) ** -0.5, 0.15625, ((1, 2),))
    decoder_second = normal_values(key_list[19], (LATENT, LATENT), LATENT ** -0.5, 0.25, ((0, 2),))
    decoder_gain = jnp.clip(1.0 + 0.18 * jax.random.normal(key_list[20], (LATENT,), jnp.float32), 0.1, 1.9)
    grid_first = normal_values(key_list[21], (2 * LATENT, LATENT), (2 * LATENT) ** -0.5, 0.1875, ((1, 2),))
    grid_second = normal_values(key_list[22], (LATENT, LATENT), LATENT ** -0.5, 0.25, ((0, 2),))
    grid_gain = jnp.clip(1.0 + 0.18 * jax.random.normal(key_list[23], (LATENT,), jnp.float32), 0.1, 1.9)
    return dict(mesh_nodes=mesh_nodes, mesh_edges=mesh_edges, grid_nodes=grid_nodes, decoder_edges=decoder_edges, mesh_sender=mesh_sender, mesh_window=mesh_window, mesh_segment=mesh_segment, mesh_lists=mesh_lists, decoder_sender=decoder_sender, decoder_window=decoder_window, decoder_segment=decoder_segment, decoder_lists=decoder_lists, edge_first=edge_first, edge_second=edge_second, edge_gain=edge_gain, node_first=node_first, node_second=node_second, node_gain=node_gain, decoder_first=decoder_first, decoder_second=decoder_second, decoder_gain=decoder_gain, grid_first=grid_first, grid_second=grid_second, grid_gain=grid_gain)


def layer_norm(values, gain):
    average = lax.optimization_barrier(jnp.mean(values, axis=-1, keepdims=True))
    centered = values - average
    variance = lax.optimization_barrier(jnp.mean(centered * centered, axis=-1, keepdims=True))
    return centered * lax.rsqrt(variance + 1e-05) * gain.astype(jnp.float32)

def perceptron(inputs, first, second, gain):
    hidden = jax.nn.silu(jnp.dot(inputs, first, preferred_element_type=jnp.float32)).astype(jnp.bfloat16)
    return layer_norm(jnp.dot(hidden, second, preferred_element_type=jnp.float32), gain)

def reference(mesh_nodes, mesh_edges, grid_nodes, decoder_edges, mesh_sender, mesh_window, mesh_segment, mesh_lists, decoder_sender, decoder_window, decoder_segment, decoder_lists, edge_first, edge_second, edge_gain, node_first, node_second, node_gain, decoder_first, decoder_second, decoder_gain, grid_first, grid_second, grid_gain):
    device = jnp.arange(N_DOM * EDGE_DEV, dtype=jnp.int32) // EDGE_DEV
    own_slot = mesh_sender < MESH_DEV
    remote_slot = jnp.maximum(mesh_sender - MESH_DEV, 0)
    source = remote_slot // MESH_CAP
    column = device * MESH_CAP + remote_slot % MESH_CAP
    remote_row = mesh_lists[source, column]
    sender_rows = jnp.where(own_slot, device * MESH_DEV + mesh_sender, source * MESH_DEV + remote_row).astype(jnp.int32)
    is_live = (mesh_segment < BLOCK).astype(jnp.float32)
    local_receiver = jnp.minimum(jnp.repeat(mesh_window, BLOCK) + mesh_segment, MESH_DEV - 1)
    receiver_rows = (device * MESH_DEV + local_receiver).astype(jnp.int32)
    inputs = jnp.concatenate([mesh_edges, mesh_nodes[sender_rows], mesh_nodes[receiver_rows]], axis=1)
    message = (mesh_edges.astype(jnp.float32) + perceptron(inputs, edge_first, edge_second, edge_gain)).astype(jnp.bfloat16)
    weighted = message.astype(jnp.float32) * is_live[:, None]
    collected = jax.ops.segment_sum(weighted, receiver_rows, num_segments=MESH_DEV * N_DOM).astype(jnp.bfloat16)
    node_inputs = jnp.concatenate([mesh_nodes, collected], axis=1)
    mesh_out = (mesh_nodes.astype(jnp.float32) + perceptron(node_inputs, node_first, node_second, node_gain)).astype(jnp.bfloat16)
    slab = jnp.arange(N_DOM * LINK_DEV, dtype=jnp.int32) // LINK_DEV
    anchor = decoder_sender // GRID_CAP
    place = slab * GRID_CAP + decoder_sender % GRID_CAP
    link_senders = (anchor * MESH_DEV + decoder_lists[anchor, place]).astype(jnp.int32)
    link_live = (decoder_segment < BLOCK).astype(jnp.float32)
    grid_receiver = jnp.minimum(jnp.repeat(decoder_window, BLOCK) + decoder_segment, GRID_DEV - 1)
    grid_rows = (slab * GRID_DEV + grid_receiver).astype(jnp.int32)
    link_inputs = jnp.concatenate([decoder_edges, mesh_out[link_senders], grid_nodes[grid_rows]], axis=1)
    link_message = (decoder_edges.astype(jnp.float32) + perceptron(link_inputs, decoder_first, decoder_second, decoder_gain)).astype(jnp.bfloat16)
    arriving = jax.ops.segment_sum(link_message.astype(jnp.float32) * link_live[:, None], grid_rows, num_segments=GRID_DEV * N_DOM).astype(jnp.bfloat16)
    grid_inputs = jnp.concatenate([grid_nodes, arriving], axis=1)
    grid_out = (grid_nodes.astype(jnp.float32) + perceptron(grid_inputs, grid_first, grid_second, grid_gain)).astype(jnp.bfloat16)
    return (mesh_out, grid_out)
```

```python
import functools

import jax
import jax.numpy as jnp
from jax import lax
from jax.experimental import pallas as pl
from jax.experimental.pallas import tpu as pltpu
from jax.sharding import PartitionSpec as P

BLOCK = 128
LANES = 128
SLOT = 16
MESH = pl.DeviceIdType.MESH
F32 = jnp.float32
BF16 = jnp.bfloat16


def dot(a, b):
    return jnp.dot(a, b, preferred_element_type=F32)


def silu(v):
    half = 0.5 * v
    return (half * jnp.tanh(half) + half).astype(BF16)


def norm_scale(values):
    average = jnp.mean(values, axis=-1, keepdims=True)
    centered = values - average
    variance = jnp.mean(centered * centered, axis=-1, keepdims=True)
    return centered * lax.rsqrt(variance + 1e-05)


def every(count, body):
    if count <= 16:
        for i in range(count):
            body(i)
    else:

        def step(i, carry):
            body(i)
            return carry

        lax.fori_loop(0, count, step, 0)


def iota(shape, dim):
    return lax.broadcasted_iota(jnp.int32, shape, dim)


def kernel(n, *refs):
    (
        nodes_in, edges_in, grid_in, links_in,
        sender_in, window_ref, segment_in, lists_in,
        dsender_in, dwindow_ref, dsegment_in, dlists_in,
        ef_in, es_in, eg_in, nf_in, ns_in, ng_in,
        df_in, ds_in, dg_in, gf_in, gs_in, gg_in,
        mesh_out, grid_out,
        nodes, edges, grid, links,
        sender, segment, lists, dsender, dsegment, dlists,
        ef, es, eg, nf, ns, ng, df, ds, dg, gf, gs, gg,
        send1, recv1, send2, recv2, mesh_full, grid_full,
        local_sem, feat_send, feat_recv, small_sem,
        a_send, a_recv, b_send, b_recv, out_sem,
    ) = refs
    me = lax.axis_index("dom")
    core = lax.axis_index("feat")
    other = 1 - core
    width = nodes_in.shape[1]
    mesh_count = nodes_in.shape[0]
    grid_count = grid_in.shape[0]
    edge_count = edges_in.shape[0]
    latent = 2 * width
    chunks = latent // LANES

    def column_half(ref, c):
        return ref.at[:, pl.ds(pl.multiple_of(c * width, width), width)]

    def row_half(ref, c):
        return ref.at[pl.ds(pl.multiple_of(c * width, width), width), :]

    barrier = pltpu.get_barrier_semaphore()
    pl.semaphore_signal(barrier, inc=1, device_id={"feat": other}, device_id_type=MESH)
    every(
        n - 1,
        lambda i: pl.semaphore_signal(
            barrier, inc=1, device_id={"dom": lax.rem(me + i + 1, n)}, device_id_type=MESH
        ),
    )

    shared = (
        (nodes_in, nodes, column_half),
        (ef_in, ef, column_half),
        (edges_in, edges, column_half),
        (es_in, es, row_half),
        (nf_in, nf, column_half),
        (ns_in, ns, row_half),
        (links_in, links, column_half),
        (grid_in, grid, column_half),
        (df_in, df, column_half),
        (ds_in, ds, row_half),
        (gf_in, gf, column_half),
        (gs_in, gs, row_half),
    )
    small = (
        (sender_in, sender), (segment_in, segment), (lists_in, lists),
        (dsender_in, dsender), (dsegment_in, dsegment), (dlists_in, dlists),
        (eg_in, eg), (ng_in, ng), (dg_in, dg), (gg_in, gg),
    )
    own = []
    far = []
    for i, (src, dst, half) in enumerate(shared):
        own.append(pltpu.make_async_copy(src, half(dst, core), local_sem.at[i]))
        far.append(
            pltpu.make_async_remote_copy(
                src_ref=src,
                dst_ref=half(dst, core),
                send_sem=feat_send.at[i],
                recv_sem=feat_recv.at[i],
                device_id={"feat": other},
                device_id_type=MESH,
            )
        )
    near = [
        pltpu.make_async_copy(src, dst, small_sem.at[i]) for i, (src, dst) in enumerate(small)
    ]
    own[0].start()
    for copy in near:
        copy.start()
    for copy in own[1:]:
        copy.start()
    pl.semaphore_wait(barrier, n)
    for copy in far:
        copy.start()

    def arrived(*which):
        for i in which:
            own[i].wait()
            far[i].wait_recv()

    def exchange(send, recv, send_sem, recv_sem, where, at):
        return pltpu.make_async_remote_copy(
            src_ref=send.at[where],
            dst_ref=recv.at[at],
            send_sem=send_sem.at[where],
            recv_sem=recv_sem.at[at],
            device_id={"dom": where},
            device_id_type=MESH,
        )

    def send_listed(table, list_row, send, recv, send_sem, recv_sem):
        cap = list_row.shape[1] // n
        rows = n * SLOT
        shape = (rows, n * cap)
        r = iota(shape, 0)
        wanted = (r // SLOT) * cap + r % cap
        picked = jnp.sum(
            jnp.where(iota(shape, 1) == wanted, list_row, 0).astype(F32), axis=1, keepdims=True
        ).astype(jnp.int32)
        one_hot = (iota((rows, mesh_count), 1) == picked).astype(BF16)
        whole = dot(one_hot, table)
        chunk = (iota((rows, LANES), 0) % SLOT) // cap
        packed = jnp.zeros((rows, LANES), F32)
        for j in range(chunks):
            packed = jnp.where(chunk == j, whole[:, j * LANES : (j + 1) * LANES], packed)
        packed = packed.astype(BF16).reshape(n, SLOT, LANES)
        send[...] = packed
        every(
            n - 1,
            lambda i: exchange(
                send, recv, send_sem, recv_sem, lax.rem(me + i + 1, n), me
            ).start(),
        )
        recv[me] = send[me]

    def receive_listed(recv, send, send_sem, recv_sem, cap, weights):
        def wait(i):
            q = lax.rem(me + i + 1, n)
            exchange(send, recv, send_sem, recv_sem, q, q).wait_recv()

        every(n - 1, wait)
        rows = n * SLOT
        packed = recv[...].reshape(rows, LANES).astype(F32)
        chunk = (iota((rows, LANES), 0) % SLOT) // cap
        spread = jnp.concatenate(
            [jnp.where(chunk == j, packed, 0.0) for j in range(chunks)], axis=1
        ).astype(BF16)
        return dot(spread, weights).astype(BF16)

    def slot_key(cap):
        r = iota((1, n * SLOT), 1)
        key = (r // SLOT) * cap + r % cap
        return jnp.where(r % SLOT < chunks * cap, key, -1)

    for copy in near:
        copy.wait()

    def receivers(segment_row, window):
        lane_block = iota((1, edge_count), 1) // BLOCK
        first = jnp.zeros((1, edge_count), jnp.int32)
        for k in range(edge_count // BLOCK):
            first = jnp.where(lane_block == k, window[k], first)
        return jnp.where(segment_row < BLOCK, first + segment_row, -1)

    receiver = receivers(segment[...], window_ref)
    dreceiver = receivers(dsegment[...], dwindow_ref)
    which = iota((8, edge_count), 0)
    rows = jnp.where(
        which == 0,
        sender[...],
        jnp.where(which == 1, receiver, jnp.where(which == 2, dsender[...], dreceiver)),
    )
    columns = rows.astype(F32).T.astype(jnp.int32)
    sender_col, receiver_col = columns[:, 0:1], columns[:, 1:2]
    dsender_col, dreceiver_col = columns[:, 2:3], columns[:, 3:4]

    arrived(0)
    send_listed(nodes[...], lists[...], send1, recv1, a_send, a_recv)

    mesh_cap = lists_in.shape[1] // n
    grid_cap = dlists_in.shape[1] // n
    arrived(1)
    from_sender = dot(nodes[...], ef[latent : 2 * latent, :]).astype(BF16)
    from_receiver = dot(nodes[...], ef[2 * latent : 3 * latent, :]).astype(BF16)
    node_lane = iota((edge_count, mesh_count), 1)
    pick_sender = (node_lane == sender_col).astype(BF16)
    pick_receiver = (node_lane == receiver_col).astype(BF16)
    pre = dot(pick_sender, from_sender) + dot(pick_receiver, from_receiver)
    arrived(2)
    pre = pre + dot(edges[...], ef[0:latent, :])
    table = receive_listed(recv1, send1, a_send, a_recv, mesh_cap, ef[latent : 2 * latent, :])
    pick_slot = (slot_key(mesh_cap) == sender_col - mesh_count).astype(BF16)
    hidden = silu(pre + dot(pick_slot, table))
    arrived(3)
    message = (
        edges[...].astype(F32) + norm_scale(dot(hidden, es[...])) * eg[...]
    ).astype(BF16)
    gather = (iota((mesh_count, edge_count), 0) == receiver).astype(BF16)
    collected = dot(gather, message).astype(BF16)

    arrived(4)
    hidden = silu(dot(nodes[...], nf[0:latent, :]) + dot(collected, nf[latent : 2 * latent, :]))
    arrived(5)
    updated = (nodes[...].astype(F32) + norm_scale(dot(hidden, ns[...])) * ng[...]).astype(BF16)
    mesh_full[...] = updated
    send_listed(updated, dlists[...], send2, recv2, b_send, b_recv)
    put_mesh = pltpu.make_async_copy(column_half(mesh_full, core), mesh_out, out_sem.at[0])
    put_mesh.start()

    arrived(6, 7, 8)
    from_grid = dot(grid[...], df[2 * latent : 3 * latent, :]).astype(BF16)
    grid_lane = iota((edge_count, grid_count), 1)
    pick_grid = (grid_lane == dreceiver_col).astype(BF16)
    pre = dot(links[...], df[0:latent, :]) + dot(pick_grid, from_grid)
    arrived(10)
    grid_pre = dot(grid[...], gf[0:latent, :])
    table = receive_listed(recv2, send2, b_send, b_recv, grid_cap, df[latent : 2 * latent, :])
    pick_slot = (slot_key(grid_cap) == dsender_col).astype(BF16)
    hidden = silu(pre + dot(pick_slot, table))
    arrived(9)
    message = (
        links[...].astype(F32) + norm_scale(dot(hidden, ds[...])) * dg[...]
    ).astype(BF16)
    gather = (iota((grid_count, edge_count), 0) == dreceiver).astype(BF16)
    collected = dot(gather, message).astype(BF16)

    hidden = silu(grid_pre + dot(collected, gf[latent : 2 * latent, :]))
    arrived(11)
    grid_full[...] = (
        grid[...].astype(F32) + norm_scale(dot(hidden, gs[...])) * gg[...]
    ).astype(BF16)
    put_grid = pltpu.make_async_copy(column_half(grid_full, core), grid_out, out_sem.at[1])
    put_grid.start()

    for copy in far:
        copy.wait_send()

    def sent(i):
        q = lax.rem(me + i + 1, n)
        exchange(send1, recv1, a_send, a_recv, q, q).wait_send()
        exchange(send2, recv2, b_send, b_recv, q, q).wait_send()

    every(n - 1, sent)
    put_mesh.wait()
    put_grid.wait()


def local(n, *args):
    args = list(args)
    for i in (4, 6, 8, 10, 14, 17, 20, 23):
        args[i] = args[i].reshape(1, -1)
    width = args[0].shape[1]
    latent = 2 * width
    any_spec = pl.BlockSpec(memory_space=pl.ANY)
    smem = pl.BlockSpec(memory_space=pltpu.SMEM)
    in_specs = [any_spec] * len(args)
    in_specs[5] = smem
    in_specs[9] = smem

    def whole_columns(a):
        return pltpu.VMEM((a.shape[0], latent), a.dtype)

    def whole_rows(a):
        return pltpu.VMEM((latent, a.shape[1]), a.dtype)

    def same(a):
        return pltpu.VMEM(a.shape, a.dtype)

    slots = pltpu.VMEM((n, SLOT, LANES), BF16)
    dma = pltpu.SemaphoreType.DMA
    return pl.pallas_call(
        functools.partial(kernel, n),
        out_shape=(
            jax.ShapeDtypeStruct(args[0].shape, BF16),
            jax.ShapeDtypeStruct(args[2].shape, BF16),
        ),
        in_specs=in_specs,
        out_specs=(any_spec, any_spec),
        scratch_shapes=[
            *[whole_columns(a) for a in args[0:4]],
            *[same(args[i]) for i in (4, 6, 7, 8, 10, 11)],
            whole_columns(args[12]), whole_rows(args[13]), same(args[14]),
            whole_columns(args[15]), whole_rows(args[16]), same(args[17]),
            whole_columns(args[18]), whole_rows(args[19]), same(args[20]),
            whole_columns(args[21]), whole_rows(args[22]), same(args[23]),
            slots, slots, slots, slots,
            whole_columns(args[0]), whole_columns(args[2]),
            dma((12,)), dma((12,)), dma((12,)), dma((10,)),
            dma((n,)), dma((n,)), dma((n,)), dma((n,)), dma((2,)),
        ],
        compiler_params=pltpu.CompilerParams(
            collective_id=0, has_side_effects=True, vmem_limit_bytes=56 * 1024 * 1024
        ),
        name="layer",
    )(*args)


def solution(mesh):
    rows = P(("groups", "dom"))
    split = P(("groups", "dom"), "feat")
    first, second, gain = P(None, "feat"), P("feat", None), P()
    return jax.shard_map(
        functools.partial(local, mesh.shape["dom"]),
        mesh=mesh,
        in_specs=(
            split, split, split, split,
            rows, rows, rows, P(("groups", "dom"), None),
            rows, rows, rows, P(("groups", "dom"), None),
            first, second, gain,
            first, second, gain,
            first, second, gain,
            first, second, gain,
        ),
        out_specs=(split, split),
        check_vma=False,
    )
```

```python
import functools

import jax
import jax.numpy as jnp
from jax import lax
from jax.experimental import pallas as pl
from jax.experimental.pallas import tpu as pltpu
from jax.sharding import PartitionSpec as P

BLOCK = 128
LANES = 128
SLOT = 16
MESH = pl.DeviceIdType.MESH
F32 = jnp.float32
BF16 = jnp.bfloat16


def dot(a, b):
    return jnp.dot(a, b, preferred_element_type=F32)


def silu(v):
    half = 0.5 * v
    return (half * jnp.tanh(half) + half).astype(BF16)


def norm_scale(values):
    average = jnp.mean(values, axis=-1, keepdims=True)
    centered = values - average
    variance = jnp.mean(centered * centered, axis=-1, keepdims=True)
    return centered * lax.rsqrt(variance + 1e-05)


def every(count, body):
    if count <= 16:
        for i in range(count):
            body(i)
    else:

        def step(i, carry):
            body(i)
            return carry

        lax.fori_loop(0, count, step, 0)


def iota(shape, dim):
    return lax.broadcasted_iota(jnp.int32, shape, dim)


def kernel(n, *refs):
    (
        nodes_in, edges_in, grid_in, links_in,
        sender_in, window_ref, segment_in, lists_in,
        dsender_in, dwindow_ref, dsegment_in, dlists_in,
        ef_in, es_in, eg_in, nf_in, ns_in, ng_in,
        df_in, ds_in, dg_in, gf_in, gs_in, gg_in,
        mesh_out, grid_out,
        nodes, edges, grid, links,
        sender, segment, lists, dsender, dsegment, dlists,
        ef, es, eg, nf, ns, ng, df, ds, dg, gf, gs, gg,
        send1, recv1, send2, recv2, mesh_full, grid_full,
        local_sem, feat_send, feat_recv, small_sem,
        a_send, a_recv, b_send, b_recv, out_sem,
    ) = refs
    me = lax.axis_index("dom")
    core = lax.axis_index("feat")
    other = 1 - core
    width = nodes_in.shape[1]
    mesh_count = nodes_in.shape[0]
    grid_count = grid_in.shape[0]
    edge_count = edges_in.shape[0]
    latent = 2 * width
    chunks = latent // LANES

    def column_half(ref, c):
        return ref.at[:, pl.ds(pl.multiple_of(c * width, width), width)]

    def row_half(ref, c):
        return ref.at[pl.ds(pl.multiple_of(c * width, width), width), :]

    barrier = pltpu.get_barrier_semaphore()
    pl.semaphore_signal(barrier, inc=1, device_id={"feat": other}, device_id_type=MESH)

    def greet(i):
        for c in range(2):
            pl.semaphore_signal(
                barrier,
                inc=1,
                device_id={"dom": lax.rem(me + i + 1, n), "feat": c},
                device_id_type=MESH,
            )

    every(n - 1, greet)

    shared = (
        (nodes_in, nodes, column_half),
        (ef_in, ef, column_half),
        (edges_in, edges, column_half),
        (es_in, es, row_half),
        (nf_in, nf, column_half),
        (ns_in, ns, row_half),
        (links_in, links, column_half),
        (grid_in, grid, column_half),
        (df_in, df, column_half),
        (ds_in, ds, row_half),
        (gf_in, gf, column_half),
        (gs_in, gs, row_half),
    )
    small = (
        (sender_in, sender), (segment_in, segment), (lists_in, lists),
        (dsender_in, dsender), (dsegment_in, dsegment), (dlists_in, dlists),
        (eg_in, eg), (ng_in, ng), (dg_in, dg), (gg_in, gg),
    )
    own = []
    far = []
    for i, (src, dst, half) in enumerate(shared):
        own.append(pltpu.make_async_copy(src, half(dst, core), local_sem.at[i]))
        far.append(
            pltpu.make_async_remote_copy(
                src_ref=src,
                dst_ref=half(dst, core),
                send_sem=feat_send.at[i],
                recv_sem=feat_recv.at[i],
                device_id={"feat": other},
                device_id_type=MESH,
            )
        )
    near = [
        pltpu.make_async_copy(src, dst, small_sem.at[i]) for i, (src, dst) in enumerate(small)
    ]
    own[0].start()
    for copy in near:
        copy.start()
    for copy in own[1:]:
        copy.start()

    def arrived(*which):
        for i in which:
            own[i].wait()
            far[i].wait_recv()

    def exchange(send, recv, send_sem, recv_sem, where, at):
        return pltpu.make_async_remote_copy(
            src_ref=send.at[where],
            dst_ref=recv.at[at],
            send_sem=send_sem.at[where],
            recv_sem=recv_sem.at[at],
            device_id={"dom": where},
            device_id_type=MESH,
        )

    def listed_rows(list_row):
        cap = list_row.shape[1] // n
        rows = n * SLOT
        shape = (rows, n * cap)
        r = iota(shape, 0)
        wanted = (r // SLOT) * cap + r % cap
        picked = jnp.sum(
            jnp.where(iota(shape, 1) == wanted, list_row, 0).astype(F32), axis=1, keepdims=True
        ).astype(jnp.int32)
        return (iota((rows, mesh_count), 1) == picked).astype(BF16)

    def pack_listed(whole, cap, first_chunk):
        rows = n * SLOT
        chunk = (iota((rows, LANES), 0) % SLOT) // cap - first_chunk
        packed = jnp.zeros((rows, LANES), F32)
        for j in range(whole.shape[1] // LANES):
            packed = jnp.where(chunk == j, whole[:, j * LANES : (j + 1) * LANES], packed)
        return packed.astype(BF16).reshape(n, SLOT, LANES)

    def spread_listed(packed, cap):
        rows = n * SLOT
        packed = packed.reshape(rows, LANES)
        chunk = (iota((rows, LANES), 0) % SLOT) // cap
        return jnp.concatenate(
            [jnp.where(chunk == j, packed, 0.0) for j in range(chunks)], axis=1
        ).astype(BF16)

    def half_listed(q, c, at, from_core):
        return pltpu.make_async_remote_copy(
            src_ref=send1.at[q],
            dst_ref=recv1.at[from_core, at],
            send_sem=a_send.at[c, q],
            recv_sem=a_recv.at[from_core, at],
            device_id={"dom": q, "feat": c},
            device_id_type=MESH,
        )

    def whole_listed(q, at):
        return exchange(send2, recv2, b_send, b_recv, q, at)

    def slot_key(cap):
        r = iota((1, n * SLOT), 1)
        key = (r // SLOT) * cap + r % cap
        return jnp.where(r % SLOT < chunks * cap, key, -1)

    for copy in near:
        copy.wait()

    def receivers(segment_row, window):
        lane_block = iota((1, edge_count), 1) // BLOCK
        first = jnp.zeros((1, edge_count), jnp.int32)
        for k in range(edge_count // BLOCK):
            first = jnp.where(lane_block == k, window[k], first)
        return jnp.where(segment_row < BLOCK, first + segment_row, -1)

    receiver = receivers(segment[...], window_ref)
    dreceiver = receivers(dsegment[...], dwindow_ref)
    which = iota((8, edge_count), 0)
    rows = jnp.where(
        which == 0,
        sender[...],
        jnp.where(which == 1, receiver, jnp.where(which == 2, dsender[...], dreceiver)),
    )
    columns = rows.astype(F32).T.astype(jnp.int32)
    sender_col, receiver_col = columns[:, 0:1], columns[:, 1:2]
    dsender_col, dreceiver_col = columns[:, 2:3], columns[:, 3:4]

    own[0].wait()
    half_nodes = nodes[:, pl.ds(pl.multiple_of(core * width, width), width)]
    mesh_cap = lists_in.shape[1] // n
    grid_cap = dlists_in.shape[1] // n
    send1[...] = pack_listed(
        dot(listed_rows(lists[...]), half_nodes), mesh_cap, core * (chunks // 2)
    )
    recv1[core, me] = send1[me]
    node_lane = iota((edge_count, mesh_count), 1)
    pick_sender = (node_lane == sender_col).astype(BF16)
    pick_receiver = (node_lane == receiver_col).astype(BF16)

    pl.semaphore_wait(barrier, 2 * n - 1)
    far[0].start()
    far[1].start()

    def send_halves(i):
        q = lax.rem(me + i + 1, n)
        for c in range(2):
            half_listed(q, c, me, core).start()

    every(n - 1, send_halves)
    half_listed(me, other, me, core).start()
    for copy in far[2:]:
        copy.start()

    far[0].wait_recv()
    arrived(1)
    from_sender = dot(nodes[...], ef[latent : 2 * latent, :]).astype(BF16)
    from_receiver = dot(nodes[...], ef[2 * latent : 3 * latent, :]).astype(BF16)
    pre = dot(pick_sender, from_sender) + dot(pick_receiver, from_receiver)
    arrived(2)
    pre = pre + dot(edges[...], ef[0:latent, :])
    pick_slot = (slot_key(mesh_cap) == sender_col - mesh_count).astype(BF16)
    gather = (iota((mesh_count, edge_count), 0) == receiver).astype(BF16)
    arrived(4)
    listed = listed_rows(dlists[...])
    listed_gather = dot(listed, gather).astype(BF16)
    listed_nodes = dot(listed, nodes[...])
    listed_pre = dot(listed_nodes.astype(BF16), nf[0:latent, :])

    def wait_halves(i):
        q = lax.rem(me + i + 1, n)
        for c in range(2):
            half_listed(q, c, q, c).wait_recv()

    every(n - 1, wait_halves)
    half_listed(me, other, me, other).wait_recv()
    packed = recv1[0].astype(F32) + recv1[1].astype(F32)
    table = dot(spread_listed(packed, mesh_cap), ef[latent : 2 * latent, :]).astype(BF16)
    hidden = silu(pre + dot(pick_slot, table))
    arrived(3)
    message = (
        edges[...].astype(F32) + norm_scale(dot(hidden, es[...])) * eg[...]
    ).astype(BF16)

    def update(before, first_pre, taken):
        hidden = silu(first_pre + dot(taken, nf[latent : 2 * latent, :]))
        return before + norm_scale(dot(hidden, ns[...])) * ng[...]

    arrived(5)
    listed_taken = dot(listed_gather, message).astype(BF16)
    send2[...] = pack_listed(update(listed_nodes, listed_pre, listed_taken), grid_cap, 0)
    every(n - 1, lambda i: whole_listed(lax.rem(me + i + 1, n), me).start())
    recv2[me] = send2[me]

    collected = dot(gather, message).astype(BF16)
    node_pre = dot(nodes[...], nf[0:latent, :])
    mesh_full[...] = update(nodes[...].astype(F32), node_pre, collected).astype(BF16)
    put_mesh = pltpu.make_async_copy(column_half(mesh_full, core), mesh_out, out_sem.at[0])
    put_mesh.start()

    arrived(6, 7, 8)
    from_grid = dot(grid[...], df[2 * latent : 3 * latent, :]).astype(BF16)
    grid_lane = iota((edge_count, grid_count), 1)
    pick_grid = (grid_lane == dreceiver_col).astype(BF16)
    pre = dot(links[...], df[0:latent, :]) + dot(pick_grid, from_grid)
    arrived(10)
    grid_pre = dot(grid[...], gf[0:latent, :])
    pick_slot = (slot_key(grid_cap) == dsender_col).astype(BF16)
    gather = (iota((grid_count, edge_count), 0) == dreceiver).astype(BF16)

    def wait_whole(i):
        q = lax.rem(me + i + 1, n)
        whole_listed(q, q).wait_recv()

    every(n - 1, wait_whole)
    packed = recv2[...].astype(F32)
    table = dot(spread_listed(packed, grid_cap), df[latent : 2 * latent, :]).astype(BF16)
    hidden = silu(pre + dot(pick_slot, table))
    arrived(9)
    message = (
        links[...].astype(F32) + norm_scale(dot(hidden, ds[...])) * dg[...]
    ).astype(BF16)
    collected = dot(gather, message).astype(BF16)

    hidden = silu(grid_pre + dot(collected, gf[latent : 2 * latent, :]))
    arrived(11)
    grid_full[...] = (
        grid[...].astype(F32) + norm_scale(dot(hidden, gs[...])) * gg[...]
    ).astype(BF16)
    put_grid = pltpu.make_async_copy(column_half(grid_full, core), grid_out, out_sem.at[1])
    put_grid.start()

    for copy in far:
        copy.wait_send()

    def sent(i):
        q = lax.rem(me + i + 1, n)
        for c in range(2):
            half_listed(q, c, q, c).wait_send()
        whole_listed(q, q).wait_send()

    every(n - 1, sent)
    half_listed(me, other, me, other).wait_send()
    put_mesh.wait()
    put_grid.wait()


def place(mesh_in, grid_in, mesh_out, grid_out, mesh_held, grid_held, sem):
    take = (
        pltpu.make_async_copy(mesh_in, mesh_held, sem.at[0]),
        pltpu.make_async_copy(grid_in, grid_held, sem.at[1]),
    )
    put = (
        pltpu.make_async_copy(mesh_held, mesh_out, sem.at[2]),
        pltpu.make_async_copy(grid_held, grid_out, sem.at[3]),
    )
    for copy in take:
        copy.start()
    for first, second in zip(take, put):
        first.wait()
        second.start()
    for copy in put:
        copy.wait()


def local(n, *args):
    args = list(args)
    for i in (4, 6, 8, 10, 14, 17, 20, 23):
        args[i] = args[i].reshape(1, -1)
    width = args[0].shape[1]
    latent = 2 * width
    any_spec = pl.BlockSpec(memory_space=pl.ANY)
    smem = pl.BlockSpec(memory_space=pltpu.SMEM)
    in_specs = [any_spec] * len(args)
    in_specs[5] = smem
    in_specs[9] = smem

    def whole_columns(a):
        return pltpu.VMEM((a.shape[0], latent), a.dtype)

    def whole_rows(a):
        return pltpu.VMEM((latent, a.shape[1]), a.dtype)

    def same(a):
        return pltpu.VMEM(a.shape, a.dtype)

    slots = pltpu.VMEM((n, SLOT, LANES), BF16)
    dma = pltpu.SemaphoreType.DMA
    outs = pl.pallas_call(
        functools.partial(kernel, n),
        out_shape=(
            jax.ShapeDtypeStruct(args[0].shape, BF16),
            jax.ShapeDtypeStruct(args[2].shape, BF16),
        ),
        in_specs=in_specs,
        out_specs=(any_spec, any_spec),
        scratch_shapes=[
            *[whole_columns(a) for a in args[0:4]],
            *[same(args[i]) for i in (4, 6, 7, 8, 10, 11)],
            whole_columns(args[12]), whole_rows(args[13]), same(args[14]),
            whole_columns(args[15]), whole_rows(args[16]), same(args[17]),
            whole_columns(args[18]), whole_rows(args[19]), same(args[20]),
            whole_columns(args[21]), whole_rows(args[22]), same(args[23]),
            slots, pltpu.VMEM((2, n, SLOT, LANES), BF16), slots, slots,
            whole_columns(args[0]), whole_columns(args[2]),
            dma((12,)), dma((12,)), dma((12,)), dma((10,)),
            dma((2, n)), dma((2, n)), dma((n,)), dma((n,)), dma((2,)),
        ],
        compiler_params=pltpu.CompilerParams(
            collective_id=0, has_side_effects=True, vmem_limit_bytes=56 * 1024 * 1024
        ),
        name="layer",
    )(*args)
    return pl.pallas_call(
        place,
        out_shape=tuple(jax.ShapeDtypeStruct(o.shape, o.dtype) for o in outs),
        in_specs=[any_spec, any_spec],
        out_specs=(any_spec, any_spec),
        scratch_shapes=[same(outs[0]), same(outs[1]), dma((4,))],
        name="place",
    )(*outs)


def solution(mesh):
    rows = P(("groups", "dom"))
    split = P(("groups", "dom"), "feat")
    first, second, gain = P(None, "feat"), P("feat", None), P()
    return jax.shard_map(
        functools.partial(local, mesh.shape["dom"]),
        mesh=mesh,
        in_specs=(
            split, split, split, split,
            rows, rows, rows, P(("groups", "dom"), None),
            rows, rows, rows, P(("groups", "dom"), None),
            first, second, gain,
            first, second, gain,
            first, second, gain,
            first, second, gain,
        ),
        out_specs=(split, split),
        check_vma=False,
    )
```
